32 devices in a mesh: req: 8 (over z, x), tp: 4 (over y, core).
Axes of the slice: x: 2, y: 2, z: 4, core: 2. Of those that a mesh axis runs over, the one named last changes fastest.
Arguments:
- query_heads: bfloat16 [7680, 4096], P('req', 'tp'), parts along dimension 0, may hold values from -140 to 140
- normed_key_heads: bfloat16 [7680, 512], P('req', 'tp'), parts along dimension 0, may hold values from -7 to 7
- value_rows_per_head: bfloat16 [7680, 512], P('req', 'tp'), parts along dimension 0, may hold values from -6 to 6
- residual_in: bfloat16 [7680, 2048], P(('req', 'tp')), parts along dimension 0, may hold values from -6 to 6
- out_weight: bfloat16 [4096, 2048], P('tp'), may hold values from -0.09375 to 0.09375
- norm_gain: float32 [2048], replicated, may hold values from 0.3 to 3
- gate_up: bfloat16 [2, 2, 2048, 768], P(None, None, None, 'tp'), may hold values from -0.125 to 0.125
- down_weight: bfloat16 [2, 768, 2048], P(None, 'tp'), may hold values from -0.21875 to 0.21875
- segment_ids: int32 [7680], P('req'), parts along dimension 0, may hold values from 0 to 5, never falling along the last dimension, each value on 1 to 480 neighbouring positions
- expert_ids: int32 [7680, 8], P('req'), parts along dimension 0, may hold values from 0 to 127, all different within a row; in each aligned block of 960 rows (0 to 959, 960 to 1919, ...) at most 75 rows name the same one
- gate_weights: float32 [7680, 8], P('req'), parts along dimension 0, may hold values from 0.05 to 0.8
Outputs:
- layer_out: bfloat16 [7680, 2048], P(('req', 'tp')), parts along dimension 0
The draws below stay inside these ranges and needn't reach their ends.
There are 8 independent parts, one for each index of `req`. The reference program is written for one: setup_inputs(seed, part) draws one part's arguments, and reference() takes and returns one part's arrays. A program takes and returns all parts, laid end to end along the dimension named above; an argument that names none is the same for every part. Nothing has to cross between parts.
Inputs may be any that keep to these rules, and one draw needn't show every extreme that they name: `segment_ids`: segment ids never fall along the tokens; each prompt has 1 to 480 tokens and one has exactly 480. `expert_ids`: the 8 experts of a token are distinct; no expert is chosen by more than 75 tokens of a request group, a bound that some block reaches.
All inputs are finite; a program needn't handle non-finite values.
Results may differ from the reference program's by a relative error of at most 0.0053.
Values may be sent and summed in bfloat16 or wider, within the bound.
A program may use at most 128 MiB of HBM per device.

```python
import math
import jax
import jax.numpy as jnp
import numpy as np
from jax import lax

D = 2048
QUERY_HEADS = 32
KEY_VALUE_HEADS = 4
HEAD_WIDTH = 128
EXPERTS = 128
TOP = 8
FF_E = 768
EXP_WIN = 2
PROMPTS = 6
GROUP_TOKENS = 960
SEG_MOST = 480
CAP = 75


def shared_heads(key):
    rotary_base = jax.random.fold_in(key, 4242)
    sampled_keys = jnp.clip(jax.random.normal(jax.random.fold_in(rotary_base, 1), (GROUP_TOKENS, KEY_VALUE_HEADS * HEAD_WIDTH), jnp.float32), -5.0, 5.0)
    queries_drawn = jnp.clip(jax.random.normal(jax.random.fold_in(rotary_base, 2), (GROUP_TOKENS, QUERY_HEADS * HEAD_WIDTH), jnp.float32), -5.0, 5.0)
    return (sampled_keys, queries_drawn)


def draw_query_heads(key, part):
    return shared_heads(key)[1].astype(jnp.bfloat16)


def draw_normed_key_heads(key, part):
    return shared_heads(key)[0].astype(jnp.bfloat16)


def shard_levels(own_key, dims, pieces, smallest, high):
    factor_of = 1.0
    for position, blocks in pieces:
        heights = jax.random.uniform(jax.random.fold_in(jax.random.fold_in(own_key, 6), position), (blocks,), jnp.float32, smallest / len(pieces), high / len(pieces))
        factor_of = factor_of * jnp.repeat(jnp.exp(heights), dims[position] // blocks).reshape((-1,) + (1,) * (len(dims) - 1 - position))
    return factor_of


def split_up(number_of, total, limit, lean):
    weights = [(1 << 20) // math.isqrt(rank ** lean) + 1 for rank in range(2, number_of + 1)]
    rest, holding = total - limit - (number_of - 1), [1] * (number_of - 1)
    while rest > 0:
        movable = [i for i in range(number_of - 1) if holding[i] < limit]
        mass, budget = sum([weights[i] for i in movable]), rest
        for i in movable:
            more = min(limit - holding[i], max(1, budget * weights[i] // mass), rest)
            holding[i] = holding[i] + more
            rest = rest - more
    return np.array([limit] + holding)


def ragged(own_key, amount, total, limit, lean):
    if amount == 2:
        one = jax.random.randint(own_key, (), max(1, total - limit), min(limit, total - 1) + 1)
        return jnp.stack([one, total - one])
    tallies = jnp.asarray(split_up(amount, total, limit, lean), jnp.int32)
    couples = (amount - 1) // 2
    source_of, sink = tallies[1:1 + 2 * couples:2], tallies[2:2 + 2 * couples:2]
    slack = jnp.minimum(source_of - 1, limit - sink)
    shifted = jax.random.randint(jax.random.fold_in(own_key, 1), (couples,), 0, 1 << 20) % (slack + 1)
    tallies = tallies.at[1:1 + 2 * couples:2].set(source_of - shifted).at[2:2 + 2 * couples:2].set(sink + shifted)
    return tallies[jax.random.permutation(jax.random.fold_in(own_key, 2), amount)]


def shared_out(rng, own, number, rows, amount, top, most, lean):
    ranking = jax.random.permutation(rng, amount)
    packed, usual = shares(amount, rows * top, most, lean, True), shares(amount, rows * top, most, lean, False)
    places = jnp.arange(amount)

    def named(tallies, rotation):
        used = int((tallies > 0).sum())
        fixed = max(1, used // 4)
        shifted = fixed + (places - fixed + rotation * (used - fixed)) % max(1, amount - fixed)
        return jnp.zeros((amount,), jnp.int32).at[ranking[jnp.where(places < fixed, places, shifted)]].set(jnp.asarray(tallies, jnp.int32))

    tallies = jnp.where(number % 4 == 0, named(packed, number // 4), named(usual, number - number // 4 - 1))
    mixed = jax.random.permutation(jax.random.fold_in(own, 3), amount)
    donor, sink = mixed[0:amount // 2 * 2:2], mixed[1:amount // 2 * 2:2]
    slack = jnp.minimum(tallies[donor] - 1, most - tallies[sink]) // 2
    slack = jnp.where((donor == ranking[0]) | (sink == ranking[0]) | (tallies[sink] == 0), 0, jnp.maximum(slack, 0))
    shifted = jax.random.randint(jax.random.fold_in(own, 4), (amount // 2,), 0, 1 << 20) % (slack + 1)
    tallies = tallies.at[donor].add(-shifted).at[sink].add(shifted)
    members = jnp.searchsorted(jnp.cumsum(tallies), jnp.arange(rows * top), side="right").astype(jnp.int32)
    grid = members.reshape(top, rows).T
    grid = grid[jax.random.permutation(jax.random.fold_in(own, 1), rows)]
    rotation = jax.random.randint(jax.random.fold_in(own, 2), (rows, 1), 0, top)
    return jnp.take_along_axis(grid, (jnp.arange(top)[None, :] + rotation) % top, axis=1)


def shares(number_of, total, limit, slope, full):
    portions = [(1 << 20) // math.isqrt(rank ** slope) + 1 for rank in range(1, number_of + 1)]
    largest = limit if full else min(limit, max(-(-total // number_of), total * portions[0] // sum(portions)))
    least = 1 if total - largest >= number_of - 1 else 0
    counts, surplus = [largest] + [least] * (number_of - 1), total - largest - least * (number_of - 1)
    while surplus > 0:
        free = [i for i in range(1, number_of) if counts[i] < largest] or [i for i in range(1, number_of) if counts[i] < limit]
        mass, left = sum([portions[i] for i in free]), surplus
        for i in free:
            extra = min(limit - counts[i], max(1, left * portions[i] // mass), surplus)
            counts[i] = counts[i] + extra
            surplus = surplus - extra
    return np.array(counts)


def centred(rng, shape, width, reach, split=(), held_as=jnp.bfloat16):
    drawn = jax.random.normal(rng, shape, jnp.float32) * width
    if len(split) > 0:
        drawn = shard_levels(rng, shape, split, -0.22, 0.18) * drawn
    return jnp.clip(drawn, min=-reach, max=reach).astype(held_as)


def setup_inputs(seed: int = 0, part: int = 0) -> dict:
    splits = jax.random.split(jax.random.key(seed), 12)
    own_keys = jax.random.split(jax.random.fold_in(splits[11], part), 12)
    query_heads = draw_query_heads(jax.random.fold_in(jax.random.fold_in(splits[11], part), 71), part)
    normed_key_heads = draw_normed_key_heads(jax.random.fold_in(jax.random.fold_in(splits[11], part), 71), part)
    value_rows_per_head = centred(own_keys[2], (GROUP_TOKENS, KEY_VALUE_HEADS * HEAD_WIDTH), 1.0, 6.0, ((1, 4),))
    residual_in = centred(own_keys[3], (GROUP_TOKENS, D), 1.0, 6.0, ((0, 4),))
    out_weight = centred(splits[4], (QUERY_HEADS * HEAD_WIDTH, D), (QUERY_HEADS * HEAD_WIDTH) ** -0.5, 0.09375, ((0, 4),))
    norm_gain = jnp.clip(jnp.exp(jax.random.uniform(splits[5], (D,), jnp.float32, math.log(0.3), math.log(3.0))), 0.3, 3.0)
    gate_up = centred(splits[6], (EXP_WIN, 2, D, FF_E), D ** -0.5, 0.125, ((3, 4),))
    down_weight = centred(splits[7], (EXP_WIN, FF_E, D), FF_E ** -0.5, 0.21875, ((1, 4),))
    segment_ids = jnp.searchsorted(jnp.cumsum(ragged(own_keys[8], PROMPTS, GROUP_TOKENS, SEG_MOST, 2)), jnp.arange(GROUP_TOKENS), side="right").astype(jnp.int32)
    expert_ids_keys = jax.random.split(jax.random.fold_in(own_keys[9], 1), GROUP_TOKENS // GROUP_TOKENS)
    expert_ids_turns = jax.random.permutation(jax.random.fold_in(own_keys[9], 3), GROUP_TOKENS // GROUP_TOKENS)
    expert_ids = jax.vmap(lambda own, number: shared_out(jax.random.fold_in(own_keys[9], 2), own, number, GROUP_TOKENS, EXPERTS, TOP, CAP, 2))(expert_ids_keys, expert_ids_turns).reshape((GROUP_TOKENS, TOP))
    gate_weights = jnp.clip(jnp.exp(jax.random.uniform(own_keys[10], (GROUP_TOKENS, TOP), jnp.float32, math.log(0.05), math.log(0.8))), 0.05, 0.8)
    return dict(query_heads=query_heads, normed_key_heads=normed_key_heads, value_rows_per_head=value_rows_per_head, residual_in=residual_in, out_weight=out_weight, norm_gain=norm_gain, gate_up=gate_up, down_weight=down_weight, segment_ids=segment_ids, expert_ids=expert_ids, gate_weights=gate_weights)


def positions_of(segment_ids):
    earlier = (segment_ids[None, :] < segment_ids[:, None]).astype(jnp.int32)
    return jnp.arange(segment_ids.shape[0], dtype=jnp.int32) - lax.optimization_barrier(jnp.sum(earlier, axis=1)).astype(jnp.int32)

def rotary_tables(vectors, token_positions):
    half_dim = vectors.shape[-1] // 2
    frequency = 1000000.0 ** (-jnp.arange(half_dim, dtype=jnp.float32) / half_dim)
    angles = token_positions.astype(jnp.float32)[:, None] * frequency[None, :]
    cosine = jnp.cos(angles)[:, None, :]
    sine = jnp.sin(angles)[:, None, :]
    first = vectors[..., :half_dim]
    second = vectors[..., half_dim:]
    return jnp.concatenate([first * cosine - second * sine, second * cosine + first * sine], axis=-1)

def rms_norm(hidden, gain):
    widened = hidden.astype(jnp.float32)
    factor = lax.rsqrt(lax.optimization_barrier(jnp.mean(widened * widened, axis=-1, keepdims=True)) + 1e-06)
    return (widened * factor * gain).astype(jnp.bfloat16)

def reference(query_heads, normed_key_heads, value_rows_per_head, residual_in, out_weight, norm_gain, gate_up, down_weight, segment_ids, expert_ids, gate_weights):
    item_count = segment_ids.shape[0]
    token_positions = positions_of(segment_ids)
    query_group_width = QUERY_HEADS // KEY_VALUE_HEADS
    queries = rotary_tables(query_heads.reshape(item_count, QUERY_HEADS, HEAD_WIDTH).astype(jnp.float32), token_positions).astype(jnp.bfloat16)
    keys_after_rotary = rotary_tables(normed_key_heads.reshape(item_count, KEY_VALUE_HEADS, HEAD_WIDTH).astype(jnp.float32), token_positions).astype(jnp.bfloat16)
    head_keys = jnp.repeat(keys_after_rotary, query_group_width, axis=1).transpose(1, 0, 2)
    value_per_head = jnp.repeat(value_rows_per_head.reshape(item_count, KEY_VALUE_HEADS, HEAD_WIDTH), query_group_width, axis=1).transpose(1, 0, 2)
    indices = jnp.arange(item_count)
    allowed = (segment_ids[:, None] == segment_ids[None, :]) & (indices[None, :] <= indices[:, None])
    factor = 1.0 / math.sqrt(HEAD_WIDTH)

    def one_head(operands):
        query_one, key_one, value_one = operands
        scores = jnp.dot(query_one, key_one.T, preferred_element_type=jnp.float32) * factor
        scores = jnp.where(allowed, scores, -1e+30)
        peak = lax.optimization_barrier(jnp.max(scores, axis=1, keepdims=True))
        weights = jnp.exp(scores - peak)
        weights = (weights / lax.optimization_barrier(jnp.sum(weights, axis=1, keepdims=True))).astype(jnp.bfloat16)
        return jnp.dot(weights, value_one, preferred_element_type=jnp.float32).astype(jnp.bfloat16)
    attended = lax.map(one_head, (queries.transpose(1, 0, 2), head_keys, value_per_head))
    attended = attended.transpose(1, 0, 2).reshape(item_count, QUERY_HEADS * HEAD_WIDTH)
    projected = jnp.dot(attended, out_weight, preferred_element_type=jnp.float32)
    mixed = (residual_in.astype(jnp.float32) + projected).astype(jnp.bfloat16)
    normed = rms_norm(mixed, norm_gain)
    slots = jnp.arange(EXP_WIN, dtype=jnp.int32)
    route = lax.optimization_barrier(jnp.sum(jnp.where(expert_ids[:, :, None] == slots[None, None, :], gate_weights[:, :, None], 0.0), axis=1))
    experts = jnp.zeros((item_count, D), jnp.float32)
    for expert in range(EXP_WIN):
        gate = jnp.dot(normed, gate_up[expert, 0], preferred_element_type=jnp.float32)
        upward = jnp.dot(normed, gate_up[expert, 1], preferred_element_type=jnp.float32)
        active = (jax.nn.silu(gate) * upward).astype(jnp.bfloat16)
        experts = experts + route[:, expert:expert + 1] * jnp.dot(active, down_weight[expert], preferred_element_type=jnp.float32)
    return (mixed.astype(jnp.float32) + experts).astype(jnp.bfloat16)
```

```python
import functools
import math

import jax
import jax.numpy as jnp
import ml_dtypes
import numpy as np
from jax import lax
from jax.experimental import pallas as pl
from jax.experimental.pallas import tpu as pltpu
from jax.sharding import PartitionSpec as P

QUERY_HEADS = 32
KEY_VALUE_HEADS = 4
HEAD_WIDTH = 128
EXPERTS = 128
SEG_MOST = 480
F32 = jnp.float32
BF16 = jnp.bfloat16
MASKED = -1e30
PIECES = 4
EXP2_SCALE = math.log2(math.e) / math.sqrt(HEAD_WIDTH)


def rotary_rows():
    half = HEAD_WIDTH // 2
    frequency = np.float32(1000000.0) ** (-np.arange(half, dtype=np.float32) / np.float32(half))
    angles = np.arange(SEG_MOST, dtype=np.float32)[:, None] * frequency[None, :].astype(np.float32)
    cosine, sine = np.cos(angles.astype(np.float64)), np.sin(angles.astype(np.float64))
    rows = np.concatenate([cosine, cosine, -sine, sine], axis=1).astype(np.float32)
    high = rows.astype(ml_dtypes.bfloat16)
    low = (rows - high.astype(np.float32)).astype(ml_dtypes.bfloat16)
    return np.concatenate([high, low], axis=1)


def dot(a, b):
    return jnp.dot(a, b, preferred_element_type=F32)


def dot_nt(a, b):
    return lax.dot_general(a, b, (((1,), (1,)), ((), ())), preferred_element_type=F32)


def layer_kernel(
    slots,
    row_ref, col_ref, table_ref, gain_ref, q_ref, k_ref, v_ref,
    res_hbm, ow_hbm, gu_hbm, dw_hbm,
    out_ref,
    res, ow, gu, dw, load_sem,
    q_rot, k_rot, v_ext, cs, bias_sel, bias, attended,
    sel_f, a1_send, a1_recv, a2_send, a2_recv, mixsel, xs, a_ssem, a_rsem,
    b1_send, b1_recv, b2_send, b2_recv, b3_send, b3_recv, own_f, b_ssem, b_rsem,
    y_f, c1_send, c1_recv, c2_send, c2_recv, ysum, c_ssem, c_rsem,
):
    me = lax.axis_index("tp")
    core = lax.rem(me, 2)
    chip = me // 2
    sib = chip * 2 + (1 - core)
    peer = (1 - chip) * 2 + core
    far = (1 - chip) * 2 + (1 - core)
    tokens, width = q_ref.shape
    heads = width // HEAD_WIDTH
    chunk = out_ref.shape[0]
    model = out_ref.shape[1]
    step = model // PIECES
    half = model // 2
    cap = slots // 2
    window = bias.shape[1]

    loads = [
        pltpu.make_async_copy(src, dst, load_sem.at[i])
        for i, (src, dst) in enumerate([(ow_hbm, ow), (res_hbm, res), (gu_hbm, gu), (dw_hbm, dw)])
    ]
    for load in loads:
        load.start()

    barrier = pltpu.get_barrier_semaphore()
    for other in (sib, peer):
        pl.semaphore_signal(
            barrier, inc=1, device_id={"tp": other}, device_id_type=pl.DeviceIdType.MESH
        )

    def remote(src, dst, ssem, rsem, to):
        return pltpu.make_async_remote_copy(
            src_ref=src, dst_ref=dst, send_sem=ssem, recv_sem=rsem,
            device_id={"tp": to}, device_id_type=pl.DeviceIdType.MESH,
        )

    copy_a1 = remote(a1_send, a1_recv, a_ssem.at[0], a_rsem.at[0], sib)
    copy_a2 = remote(a2_send, a2_recv, a_ssem.at[1], a_rsem.at[1], peer)
    copy_a3 = remote(mixsel.at[core], mixsel.at[core], a_ssem.at[2], a_rsem.at[2], sib)
    copy_b1 = [remote(b1_send.at[p], b1_recv.at[p], b_ssem.at[0, p], b_rsem.at[0, p], sib) for p in range(PIECES)]
    copy_b2 = [remote(b2_send.at[p], b2_recv.at[p], b_ssem.at[1, p], b_rsem.at[1, p], peer) for p in range(PIECES)]
    copy_b3 = [remote(b3_send.at[p], b3_recv.at[p], b_ssem.at[2, p], b_rsem.at[2, p], sib) for p in range(PIECES)]
    copy_c1 = remote(c1_send, c1_recv, c_ssem.at[0], c_rsem.at[0], sib)
    copy_c2 = remote(c2_send, c2_recv, c_ssem.at[1], c_rsem.at[1], peer)
    copy_c3 = remote(ysum.at[core], ysum.at[core], c_ssem.at[2], c_rsem.at[2], sib)

    token_col = lax.broadcasted_iota(jnp.int32, (tokens, 1), 0).astype(F32)
    position = token_col - col_ref[:, 0:1]
    places = lax.broadcasted_iota(jnp.int32, (tokens, SEG_MOST), 1).astype(F32)
    looked = dot((position == places).astype(BF16), table_ref[...])
    cs[...] = looked[:, : 2 * HEAD_WIDTH] + looked[:, 2 * HEAD_WIDTH :]

    def rotate(u):
        u = u.astype(F32)
        turned = pltpu.roll(u, HEAD_WIDTH // 2, 1)
        return (u * cs[:, :HEAD_WIDTH] + turned * cs[:, HEAD_WIDTH:]).astype(BF16)

    k_rot[...] = rotate(k_ref[...])
    v_ext[:, :HEAD_WIDTH] = v_ref[...]
    v_ext[:, HEAD_WIDTH:] = jnp.ones((tokens, HEAD_WIDTH), BF16)

    def rotate_head(h, carry):
        lanes = pl.ds(pl.multiple_of(h * HEAD_WIDTH, HEAD_WIDTH), HEAD_WIDTH)
        q_rot[:, lanes] = rotate(q_ref[:, lanes])
        return carry

    lax.fori_loop(0, heads, rotate_head, 0)

    start_row = row_ref[0:1, :]
    lane_tokens = lax.broadcasted_iota(jnp.int32, (cap, tokens), 1).astype(F32)
    slot_col = lax.broadcasted_iota(jnp.int32, (cap, tokens), 0).astype(F32)
    picks, routes = [], []
    for e in range(2):
        hit = row_ref[1 + e : 2 + e, :] == slot_col
        picks.append(hit.astype(F32).astype(BF16))
        routes.append(jnp.sum(jnp.where(hit, row_ref[3 + e : 4 + e, :], 0.0), axis=1, keepdims=True))
        first = jnp.sum(jnp.where(hit, start_row, 0.0), axis=1, keepdims=True)
        last = jnp.sum(jnp.where(hit, lane_tokens, 0.0), axis=1, keepdims=True)
        keep = (lane_tokens >= first) & (lane_tokens <= last)
        bias_sel[e * cap : (e + 1) * cap, :] = jnp.where(keep, 0.0, MASKED)
    pick = jnp.concatenate(picks, axis=0)
    q_sel = dot(pick, q_rot[...]).astype(BF16)

    def attend(query, keys, values, added):
        scores = dot_nt(query, keys) + added
        peak = jnp.max(scores, axis=1, keepdims=True)
        weights = jnp.exp2((scores - peak) * EXP2_SCALE).astype(BF16)
        mixed = dot(weights, values)
        return (mixed[:, :HEAD_WIDTH] / mixed[:, HEAD_WIDTH:]).astype(BF16)

    pl.semaphore_wait(barrier, 2)

    for h in range(heads):
        lanes = slice(h * HEAD_WIDTH, (h + 1) * HEAD_WIDTH)
        attended[:slots, lanes] = attend(q_sel[:, lanes], k_rot[...], v_ext[...], bias_sel[...])
    loads[0].wait()
    loads[1].wait()
    own_tokens = (lax.broadcasted_iota(jnp.int32, (slots, chunk), 1) + me * chunk).astype(F32)
    ident = jnp.sum(jnp.where(pick > 0, jnp.concatenate([lane_tokens, lane_tokens], axis=0) + 1.0, 0.0), axis=1, keepdims=True) - 1.0
    own_pick = (own_tokens == ident).astype(F32).astype(BF16)
    for p in range(PIECES):
        columns = slice(p * step, (p + 1) * step)
        share = dot(attended[:slots, :], ow[:, columns]) + dot(own_pick, res[:, columns])
        inner = p % (PIECES // 2) * step
        sel_f[p * 2 // PIECES, :, inner : inner + step] = share
    a1_send[...] = sel_f[1 - core].astype(BF16)
    copy_a1.start()

    def forward_a():
        copy_a1.wait_recv()
        a2_send[...] = (sel_f[core] + a1_recv[...].astype(F32)).astype(BF16)
        copy_a2.start()

    def attend_chunk(r, hooks):
        base = pl.multiple_of(r * chunk, 16)
        low = pl.multiple_of(jnp.maximum(r * chunk + chunk - window, 0), 16)
        first = col_ref[pl.ds(base, chunk), 0:1]
        query_at = (lax.broadcasted_iota(jnp.int32, (chunk, window), 0) + base).astype(F32)
        key_at = (lax.broadcasted_iota(jnp.int32, (chunk, window), 1) + low).astype(F32)
        bias[...] = jnp.where((key_at >= first) & (key_at <= query_at), 0.0, MASKED)

        def two_heads(i, carry):
            for s in range(2):
                lanes = pl.ds(pl.multiple_of((2 * i + s) * HEAD_WIDTH, HEAD_WIDTH), HEAD_WIDTH)
                attended[:chunk, lanes] = attend(
                    q_rot[pl.ds(base, chunk), lanes],
                    k_rot[pl.ds(low, window), :],
                    v_ext[pl.ds(low, window), :],
                    bias[...],
                )
            return carry

        quarter = heads // 4
        lax.fori_loop(0, quarter, two_heads, 0)
        hooks[0]()
        lax.fori_loop(quarter, heads // 2, two_heads, 0)
        hooks[1]()

    def project(p):
        return dot(attended[:chunk, :], ow[:, p * step : (p + 1) * step])

    def nothing():
        pass

    attend_chunk(far, (forward_a, nothing))
    for p in range(PIECES):
        b1_send[p] = project(p).astype(BF16)
        copy_b1[p].start()

    attend_chunk(peer, (nothing, nothing))
    for p in range(PIECES):
        share = project(p)
        copy_b1[p].wait_recv()
        b2_send[p] = (share + b1_recv[p].astype(F32)).astype(BF16)
        copy_b2[p].start()

    copy_a2.wait_recv()
    mixsel[core] = (a2_send[...].astype(F32) + a2_recv[...].astype(F32)).astype(BF16)
    copy_a3.start()

    def experts():
        copy_a3.wait_recv()
        left, right = mixsel[0].astype(F32), mixsel[1].astype(F32)
        mean = (jnp.sum(left * left, axis=1, keepdims=True) + jnp.sum(right * right, axis=1, keepdims=True)) / model
        scale = lax.rsqrt(mean + 1e-06)
        xs[:, :half] = (left * scale * gain_ref[:, :half]).astype(BF16)
        xs[:, half:] = (right * scale * gain_ref[:, half:]).astype(BF16)
        loads[2].wait()
        loads[3].wait()
        for e in range(2):
            rows = slice(e * cap, (e + 1) * cap)
            gate = dot(xs[rows, :], gu[e, 0])
            upward = dot(xs[rows, :], gu[e, 1])
            active = (gate / (1.0 + jnp.exp(-gate)) * upward).astype(BF16)
            for s in range(2):
                y_f[s, rows, :] = dot(active, dw[e, :, s * half : (s + 1) * half]) * routes[e]
        c1_send[...] = y_f[1 - core].astype(BF16)
        copy_c1.start()

    def forward_c():
        copy_c1.wait_recv()
        c2_send[...] = (y_f[core] + c1_recv[...].astype(F32)).astype(BF16)
        copy_c2.start()

    attend_chunk(sib, (experts, forward_c))
    for p in range(PIECES):
        b3_send[p] = project(p).astype(BF16)
        copy_b3[p].start()

    attend_chunk(me, (nothing, nothing))
    for p in range(PIECES):
        columns = slice(p * step, (p + 1) * step)
        own_f[p] = project(p) + res[:, columns].astype(F32)

    for p in range(PIECES):
        copy_b3[p].wait_recv()
        copy_b2[p].wait_recv()
        own_f[p] = own_f[p] + b3_recv[p].astype(F32) + b2_recv[p].astype(F32)

    copy_c2.wait_recv()
    ysum[core] = (c2_send[...].astype(F32) + c2_recv[...].astype(F32)).astype(BF16)
    copy_c3.start()

    mine = pl.ds(pl.multiple_of(me * chunk, 16), chunk)
    slot_lane = lax.broadcasted_iota(jnp.int32, (chunk, cap), 1).astype(F32)
    spread = [
        (col_ref[mine, 1 + e : 2 + e] == slot_lane).astype(F32).astype(BF16) for e in range(2)
    ]
    copy_c3.wait_recv()
    for p in range(PIECES):
        inner = p % (PIECES // 2) * step
        side = p * 2 // PIECES
        given = sum(
            dot(spread[e], ysum[side, e * cap : (e + 1) * cap, inner : inner + step])
            for e in range(2)
        )
        mixed = own_f[p].astype(BF16).astype(F32)
        out_ref[:, p * step : (p + 1) * step] = (mixed + given).astype(BF16)

    for copy in [copy_a1, copy_a2, copy_a3, copy_c1, copy_c2, copy_c3] + copy_b1 + copy_b2 + copy_b3:
        copy.wait_send()


def local(
    query_heads,
    normed_key_heads,
    value_rows_per_head,
    residual_in,
    out_weight,
    norm_gain,
    gate_up,
    down_weight,
    segment_ids,
    expert_ids,
    gate_weights,
):
    tokens, width = query_heads.shape
    chunk, model = residual_in.shape
    capacity = tokens * expert_ids.shape[1] * 5 // (EXPERTS * 4)
    cap = -(-capacity // 16) * 16
    slots = 2 * cap
    window = min(tokens, -(-(chunk + SEG_MOST - 1) // 16) * 16)

    index = jnp.arange(tokens, dtype=jnp.int32)
    start = jnp.sum((segment_ids[:, None] < segment_ids[None, :]).astype(F32), axis=0)
    window_ids = jnp.arange(2, dtype=jnp.int32)
    named = expert_ids.T[None, :, :] == window_ids[:, None, None]
    chosen = jnp.any(named, axis=1)
    route = jnp.sum(jnp.where(named, gate_weights.T[None, :, :], 0.0), axis=1)
    before = (index[:, None] < index[None, :]).astype(BF16)
    rank = jnp.dot(chosen.astype(BF16), before, preferred_element_type=F32)
    slot = jnp.where(chosen, rank, -1.0)
    rows = jnp.concatenate([start[None, :], slot, route, jnp.zeros((3, tokens), F32)], axis=0)
    cols = rows.T

    vmem = pl.BlockSpec(memory_space=pltpu.VMEM)
    hbm = pl.BlockSpec(memory_space=pl.ANY)
    step = model // PIECES
    half = model // 2
    dma = pltpu.SemaphoreType.DMA
    pieces = (PIECES, chunk, step)
    scratch = [
        pltpu.VMEM(residual_in.shape, BF16),
        pltpu.VMEM(out_weight.shape, BF16),
        pltpu.VMEM(gate_up.shape, BF16),
        pltpu.VMEM(down_weight.shape, BF16),
        dma((4,)),
        pltpu.VMEM((tokens, width), BF16),
        pltpu.VMEM((tokens, HEAD_WIDTH), BF16),
        pltpu.VMEM((tokens, 2 * HEAD_WIDTH), BF16),
        pltpu.VMEM((tokens, 2 * HEAD_WIDTH), F32),
        pltpu.VMEM((slots, tokens), F32),
        pltpu.VMEM((chunk, window), F32),
        pltpu.VMEM((max(chunk, slots), width), BF16),
        pltpu.VMEM((2, slots, half), F32),
        pltpu.VMEM((slots, half), BF16),
        pltpu.VMEM((slots, half), BF16),
        pltpu.VMEM((slots, half), BF16),
        pltpu.VMEM((slots, half), BF16),
        pltpu.VMEM((2, slots, half), BF16),
        pltpu.VMEM((slots, model), BF16),
        dma((3,)),
        dma((3,)),
        pltpu.VMEM(pieces, BF16),
        pltpu.VMEM(pieces, BF16),
        pltpu.VMEM(pieces, BF16),
        pltpu.VMEM(pieces, BF16),
        pltpu.VMEM(pieces, BF16),
        pltpu.VMEM(pieces, BF16),
        pltpu.VMEM(pieces, F32),
        dma((3, PIECES)),
        dma((3, PIECES)),
        pltpu.VMEM((2, slots, half), F32),
        pltpu.VMEM((slots, half), BF16),
        pltpu.VMEM((slots, half), BF16),
        pltpu.VMEM((slots, half), BF16),
        pltpu.VMEM((slots, half), BF16),
        pltpu.VMEM((2, slots, half), BF16),
        dma((3,)),
        dma((3,)),
    ]
    return pl.pallas_call(
        functools.partial(layer_kernel, slots),
        out_shape=jax.ShapeDtypeStruct((chunk, model), BF16),
        in_specs=[vmem] * 7 + [hbm] * 4,
        out_specs=vmem,
        scratch_shapes=scratch,
        compiler_params=pltpu.CompilerParams(
            collective_id=0, has_side_effects=True, vmem_limit_bytes=56 * 1024 * 1024
        ),
        cost_estimate=pl.CostEstimate(
            flops=14_000_000_000, bytes_accessed=14_000_000, transcendentals=7_000_000
        ),
    )(
        rows, cols, jnp.asarray(rotary_rows()), norm_gain[None, :],
        query_heads, normed_key_heads, value_rows_per_head,
        residual_in, out_weight, gate_up, down_weight,
    )


def solution(mesh):
    placed = (
        P("req", "tp"),
        P("req", "tp"),
        P("req", "tp"),
        P(("req", "tp"), None),
        P("tp", None),
        P(),
        P(None, None, None, "tp"),
        P(None, "tp", None),
        P("req"),
        P("req", None),
        P("req", None),
    )
    return jax.shard_map(
        local, mesh=mesh, in_specs=placed, out_specs=P(("req", "tp"), None), check_vma=False
    )
```

```python
import functools
import math

import jax
import jax.numpy as jnp
import numpy as np
from jax import lax
from jax.experimental import pallas as pl
from jax.experimental.pallas import tpu as pltpu
from jax.sharding import PartitionSpec as P

QUERY_HEADS = 32
KEY_VALUE_HEADS = 4
HEAD_WIDTH = 128
EXPERTS = 128
SEG_MOST = 480
F32 = jnp.float32
BF16 = jnp.bfloat16
MASKED = -1e30
PIECES = 4
HEADS_AT_ONCE = 4
COPIES = 5
EXP2_SCALE = math.log2(math.e) / math.sqrt(HEAD_WIDTH)


def rotary_rows():
    half = HEAD_WIDTH // 2
    frequency = np.float32(1000000.0) ** (-np.arange(half, dtype=np.float32) / np.float32(half))
    angles = np.arange(SEG_MOST, dtype=np.float32)[:, None] * frequency[None, :].astype(np.float32)
    cosine, sine = np.cos(angles.astype(np.float64)), np.sin(angles.astype(np.float64))
    return np.concatenate([cosine, cosine, -sine, sine], axis=1).astype(np.float32)


def dot(a, b):
    return jnp.dot(a, b, preferred_element_type=F32)


def dot_nt(a, b):
    return lax.dot_general(a, b, (((1,), (1,)), ((), ())), preferred_element_type=F32)


def layer_kernel(
    slots, parts,
    seg_ref, ids_ref, gw_ref, table_ref, gain_ref, k_ref, v_ref,
    q_hbm, res_hbm, ow_hbm, gu_hbm, dw_hbm,
    out_ref,
    q, res, ow, gu, dw, load_sem,
    rows_ref, cols_ref, k_rot, v_ext, cs, bias_sel, bias, attended,
    sel_f, a1_send, a1_recv, a2_send, a2_recv, mixsel, xs, a_ssem, a_rsem,
    b1_send, b1_recv, b2_send, b2_recv, b3_send, b3_recv, own_f, b_ssem, b_rsem,
    y_f, c1_send, c1_recv, c2_send, c2_recv, ysum, c_ssem, c_rsem,
):
    me = lax.axis_index("tp")
    core = lax.rem(me, 2)
    chip = me // 2
    sib = chip * 2 + (1 - core)
    peer = (1 - chip) * 2 + core
    far = (1 - chip) * 2 + (1 - core)
    tokens, width = q.shape
    heads = width // HEAD_WIDTH
    chunk, model = out_ref.shape
    step = model // PIECES
    half = model // 2
    cap = slots // 2

    loads = [
        pltpu.make_async_copy(src, dst, load_sem.at[i])
        for i, (src, dst) in enumerate(
            [(q_hbm, q), (ow_hbm, ow), (res_hbm, res), (gu_hbm, gu), (dw_hbm, dw)]
        )
    ]
    for load in loads:
        load.start()

    barrier = pltpu.get_barrier_semaphore()
    for other in (sib, peer):
        pl.semaphore_signal(
            barrier, inc=1, device_id={"tp": other}, device_id_type=pl.DeviceIdType.MESH
        )

    def remote(src, dst, ssem, rsem, to):
        return pltpu.make_async_remote_copy(
            src_ref=src, dst_ref=dst, send_sem=ssem, recv_sem=rsem,
            device_id={"tp": to}, device_id_type=pl.DeviceIdType.MESH,
        )

    def remote_parts(i, src, dst, to):
        return [
            [
                remote(
                    src.at[s, p, pl.ds(0, rows)], dst.at[s, p, pl.ds(0, rows)],
                    b_ssem.at[i, s, p], b_rsem.at[i, s, p], to,
                )
                for p in range(PIECES)
            ]
            for s, (_, rows, _) in enumerate(parts)
        ]

    copy_a1 = remote(a1_send, a1_recv, a_ssem.at[0], a_rsem.at[0], sib)
    copy_a2 = remote(a2_send, a2_recv, a_ssem.at[1], a_rsem.at[1], peer)
    copy_a3 = remote(mixsel.at[core], mixsel.at[core], a_ssem.at[2], a_rsem.at[2], sib)
    copy_b1 = remote_parts(0, b1_send, b1_recv, sib)
    copy_b2 = remote_parts(1, b2_send, b2_recv, peer)
    copy_b3 = remote_parts(2, b3_send, b3_recv, sib)
    copy_c1 = remote(c1_send, c1_recv, c_ssem.at[0], c_rsem.at[0], sib)
    copy_c2 = remote(c2_send, c2_recv, c_ssem.at[1], c_rsem.at[1], peer)
    copy_c3 = remote(ysum.at[core], ysum.at[core], c_ssem.at[2], c_rsem.at[2], sib)

    seg = seg_ref[...]
    prompts = lax.broadcasted_iota(jnp.int32, (8, tokens), 0)
    starts = jnp.sum((seg < prompts).astype(F32), axis=1, keepdims=True)
    start_row = jnp.sum(jnp.where(seg == prompts, starts, 0.0), axis=0, keepdims=True)
    named = [ids_ref[...] == e for e in range(2)]
    chosen = [jnp.max(hit.astype(F32), axis=0, keepdims=True) for hit in named]
    route_rows = [jnp.sum(jnp.where(hit, gw_ref[...], 0.0), axis=0, keepdims=True) for hit in named]
    expert_at = lax.broadcasted_iota(jnp.int32, (16, tokens), 0)
    chosen = jnp.where(expert_at == 0, chosen[0], jnp.where(expert_at == 1, chosen[1], 0.0))
    upper = (
        lax.broadcasted_iota(jnp.int32, (128, 128), 0)
        < lax.broadcasted_iota(jnp.int32, (128, 128), 1)
    ).astype(F32).astype(BF16)
    rows_ref[...] = jnp.zeros_like(rows_ref)
    total = jnp.zeros((16, 1), F32)
    for low in range(0, tokens, 128):
        wide = min(128, tokens - low)
        block = chosen[:, low : low + wide]
        rank = dot(block.astype(BF16), upper[:wide, :wide]) + total
        total = total + jnp.sum(block, axis=1, keepdims=True)
        slot = jnp.where(block > 0, rank, -1.0)[:8]
        line = lax.broadcasted_iota(jnp.int32, (8, wide), 0)
        rows_ref[:, low : low + wide] = jnp.where(line == 2, start_row[:, low : low + wide], slot)
    cols_ref[...] = rows_ref[...].T

    table = table_ref[...]
    high = table.astype(BF16)
    low = (table - high.astype(F32)).astype(BF16)

    def rotary(position):
        places = lax.broadcasted_iota(jnp.int32, (position.shape[0], SEG_MOST), 1).astype(F32)
        at = (position == places).astype(F32).astype(BF16)
        return dot(at, high) + dot(at, low)

    def rotate(u, turn):
        u = u.astype(F32)
        turned = pltpu.roll(u, HEAD_WIDTH // 2, 1)
        return (u * turn[:, :HEAD_WIDTH] + turned * turn[:, HEAD_WIDTH:]).astype(BF16)

    token_col = lax.broadcasted_iota(jnp.int32, (tokens, 1), 0).astype(F32)
    cs[...] = rotary(token_col - cols_ref[:tokens, 2:3])
    k_rot[...] = rotate(k_ref[...], cs[...])
    v_ext[:, :HEAD_WIDTH] = v_ref[...]
    v_ext[:, HEAD_WIDTH:] = jnp.ones((tokens, HEAD_WIDTH), BF16)

    lane_tokens = lax.broadcasted_iota(jnp.int32, (cap, tokens), 1).astype(F32)
    slot_col = lax.broadcasted_iota(jnp.int32, (cap, tokens), 0).astype(F32)
    picks, routes, firsts, lasts, idents = [], [], [], [], []
    for e in range(2):
        hit = rows_ref[e : e + 1, :tokens] == slot_col
        picks.append(hit.astype(F32).astype(BF16))
        routes.append(jnp.sum(jnp.where(hit, route_rows[e], 0.0), axis=1, keepdims=True))
        first = jnp.sum(jnp.where(hit, start_row, 0.0), axis=1, keepdims=True)
        found = jnp.sum(jnp.where(hit, lane_tokens + 1.0, 0.0), axis=1, keepdims=True)
        last = jnp.maximum(found - 1.0, 0.0)
        keep = (lane_tokens >= first) & (lane_tokens <= last)
        bias_sel[e * cap : (e + 1) * cap, :] = jnp.where(keep, 0.0, MASKED)
        firsts.append(first)
        lasts.append(last)
        idents.append(found - 1.0)
    pick = jnp.concatenate(picks, axis=0)
    turn_sel = rotary(jnp.concatenate(lasts, axis=0) - jnp.concatenate(firsts, axis=0))
    loads[0].wait()
    q_sel = dot(pick, q[...])

    def attend(query, keys, values, added):
        scores = dot_nt(query, keys) + added
        peak = jnp.max(scores, axis=1, keepdims=True)
        weights = jnp.exp2((scores - peak) * EXP2_SCALE).astype(BF16)
        mixed = dot(weights, values)
        return (mixed[:, :HEAD_WIDTH] / mixed[:, HEAD_WIDTH:]).astype(BF16)

    for h in range(heads):
        lanes = slice(h * HEAD_WIDTH, (h + 1) * HEAD_WIDTH)
        attended[:slots, lanes] = attend(
            rotate(q_sel[:, lanes], turn_sel), k_rot[...], v_ext[...], bias_sel[...]
        )
    loads[1].wait()
    loads[2].wait()
    own_tokens = (lax.broadcasted_iota(jnp.int32, (slots, chunk), 1) + me * chunk).astype(F32)
    own_pick = (own_tokens == jnp.concatenate(idents, axis=0)).astype(F32).astype(BF16)

    def chosen_share(side):
        columns = pl.ds(pl.multiple_of(side * half, half), half)
        return dot(attended[:slots, :], ow[:, columns]) + dot(own_pick, res[:, columns])

    a1_send[...] = chosen_share(1 - core).astype(BF16)
    pl.semaphore_wait(barrier, 2)
    copy_a1.start()
    sel_f[...] = chosen_share(core)

    def forward_a():
        copy_a1.wait_recv()
        a2_send[...] = (sel_f[...] + a1_recv[...].astype(F32)).astype(BF16)
        copy_a2.start()

    def attend_part(r, s, hooks=()):
        offset, rows, window = parts[s]
        base = pl.multiple_of(r * chunk + offset, 16)
        low = pl.multiple_of(jnp.maximum(r * chunk + (offset + rows - window), 0), 16)
        first = cols_ref[pl.ds(base, rows), 2:3]
        query_at = (lax.broadcasted_iota(jnp.int32, (rows, window), 0) + base).astype(F32)
        key_at = (lax.broadcasted_iota(jnp.int32, (rows, window), 1) + low).astype(F32)
        bias[:rows, :window] = jnp.where((key_at >= first) & (key_at <= query_at), 0.0, MASKED)

        def some_heads(i, carry):
            for n in range(HEADS_AT_ONCE):
                h = i * HEADS_AT_ONCE + n
                lanes = pl.ds(pl.multiple_of(h * HEAD_WIDTH, HEAD_WIDTH), HEAD_WIDTH)
                attended[:rows, lanes] = attend(
                    rotate(q[pl.ds(base, rows), lanes], cs[pl.ds(base, rows), :]),
                    k_rot[pl.ds(low, window), :],
                    v_ext[pl.ds(low, window), :],
                    bias[:rows, :window],
                )
            return carry

        turns = heads // HEADS_AT_ONCE
        if hooks:
            lax.fori_loop(0, turns // 2, some_heads, 0)
            hooks[0]()
            lax.fori_loop(turns // 2, turns, some_heads, 0)
            hooks[1]()
        else:
            lax.fori_loop(0, turns, some_heads, 0)

    def project(s, p):
        return dot(attended[: parts[s][1], :], ow[:, p * step : (p + 1) * step])

    def send_far(s):
        rows = parts[s][1]
        for p in range(PIECES):
            b1_send[s, p, :rows] = project(s, p).astype(BF16)
            copy_b1[s][p].start()

    def send_peer(s):
        rows = parts[s][1]
        for p in range(PIECES):
            share = project(s, p)
            copy_b1[s][p].wait_recv()
            b2_send[s, p, :rows] = (share + b1_recv[s, p, :rows].astype(F32)).astype(BF16)
            copy_b2[s][p].start()

    def nothing():
        pass

    def experts():
        copy_a3.wait_recv()
        left, right = mixsel[0].astype(F32), mixsel[1].astype(F32)
        mean = (
            jnp.sum(left * left, axis=1, keepdims=True)
            + jnp.sum(right * right, axis=1, keepdims=True)
        ) / model
        scale = lax.rsqrt(mean + 1e-06)
        xs[:, :half] = (left * scale * gain_ref[:, :half]).astype(BF16)
        xs[:, half:] = (right * scale * gain_ref[:, half:]).astype(BF16)
        loads[3].wait()
        loads[4].wait()
        for e in range(2):
            rows = slice(e * cap, (e + 1) * cap)
            gate = dot_nt(xs[rows, :], gu[e, 0])
            upward = dot_nt(xs[rows, :], gu[e, 1])
            active = (gate / (1.0 + jnp.exp(-gate)) * upward).astype(BF16)
            for side in range(2):
                y_f[side, rows, :] = dot(active, dw[e, :, side * half : (side + 1) * half]) * routes[e]
        c1_send[...] = y_f[1 - core].astype(BF16)
        copy_c1.start()

    def forward_c():
        copy_c1.wait_recv()
        c2_send[...] = (y_f[core] + c1_recv[...].astype(F32)).astype(BF16)
        copy_c2.start()

    attend_part(far, 0, (forward_a, nothing))
    send_far(0)
    attend_part(peer, 0)
    send_peer(0)
    attend_part(far, 1)
    send_far(1)
    copy_a2.wait_recv()
    mixsel[core] = (a2_send[...].astype(F32) + a2_recv[...].astype(F32)).astype(BF16)
    copy_a3.start()
    attend_part(peer, 1, (experts, forward_c))
    send_peer(1)

    for s in range(len(parts)):
        attend_part(sib, s)
        for p in range(PIECES):
            b3_send[s, p, : parts[s][1]] = project(s, p).astype(BF16)
            copy_b3[s][p].start()
    for s, (offset, rows, _) in enumerate(parts):
        attend_part(me, s)
        for p in range(PIECES):
            columns = slice(p * step, (p + 1) * step)
            own_f[s, p, :rows] = project(s, p) + res[offset : offset + rows, columns].astype(F32)

    copy_c2.wait_recv()
    ysum[core] = (c2_send[...].astype(F32) + c2_recv[...].astype(F32)).astype(BF16)
    copy_c3.start()
    for s, (_, rows, _) in enumerate(parts):
        for p in range(PIECES):
            copy_b3[s][p].wait_recv()
            own_f[s, p, :rows] = own_f[s, p, :rows] + b3_recv[s, p, :rows].astype(F32)
    copy_c3.wait_recv()
    for s, (offset, rows, _) in enumerate(parts):
        mine = pl.ds(pl.multiple_of(me * chunk + offset, 16), rows)
        slot_lane = lax.broadcasted_iota(jnp.int32, (rows, cap), 1).astype(F32)
        spread = [
            (cols_ref[mine, e : e + 1] == slot_lane).astype(F32).astype(BF16) for e in range(2)
        ]
        for p in range(PIECES):
            inner = p % (PIECES // 2) * step
            side = p * 2 // PIECES
            given = sum(
                dot(spread[e], ysum[side, e * cap : (e + 1) * cap, inner : inner + step])
                for e in range(2)
            )
            copy_b2[s][p].wait_recv()
            mixed = own_f[s, p, :rows] + b2_recv[s, p, :rows].astype(F32)
            mixed = mixed.astype(BF16).astype(F32)
            out_ref[offset : offset + rows, p * step : (p + 1) * step] = (mixed + given).astype(BF16)

    for copy in [copy_a1, copy_a2, copy_a3, copy_c1, copy_c2, copy_c3]:
        copy.wait_send()
    for copies in copy_b1 + copy_b2 + copy_b3:
        for copy in copies:
            copy.wait_send()


def hand_over(src, dst, sem):
    rows = src.shape[0] // COPIES
    copies = [
        pltpu.make_async_copy(
            src.at[pl.ds(i * rows, rows)], dst.at[pl.ds(i * rows, rows)], sem.at[i]
        )
        for i in range(COPIES)
    ]
    for copy in copies:
        copy.start()
    for copy in copies:
        copy.wait()


def local(
    query_heads,
    normed_key_heads,
    value_rows_per_head,
    residual_in,
    out_weight,
    norm_gain,
    gate_up,
    down_weight,
    segment_ids,
    expert_ids,
    gate_weights,
):
    tokens, width = query_heads.shape
    chunk, model = residual_in.shape
    capacity = tokens * expert_ids.shape[1] * 5 // (EXPERTS * 4)
    cap = -(-capacity // 16) * 16
    slots = 2 * cap
    first_rows = -(-chunk // 32) * 16
    parts = tuple(
        (offset, rows, min(tokens, -(-(rows + SEG_MOST - 1) // 16) * 16))
        for offset, rows in ((0, first_rows), (first_rows, chunk - first_rows))
    )
    most = max(rows for _, rows, _ in parts)
    window = max(wide for _, _, wide in parts)
    lanes = -(-tokens // 128) * 128


    vmem = pl.BlockSpec(memory_space=pltpu.VMEM)
    hbm = pl.BlockSpec(memory_space=pl.ANY)
    step = model // PIECES
    half = model // 2
    dma = pltpu.SemaphoreType.DMA
    pieces = (2, PIECES, most, step)
    gate_up = jnp.swapaxes(gate_up, 2, 3)
    scratch = [
        pltpu.VMEM((tokens, width), BF16),
        pltpu.VMEM(residual_in.shape, BF16),
        pltpu.VMEM(out_weight.shape, BF16),
        pltpu.VMEM(gate_up.shape, BF16),
        pltpu.VMEM(down_weight.shape, BF16),
        dma((5,)),
        pltpu.VMEM((8, lanes), F32),
        pltpu.VMEM((lanes, 8), F32),
        pltpu.VMEM((tokens, HEAD_WIDTH), BF16),
        pltpu.VMEM((tokens, 2 * HEAD_WIDTH), BF16),
        pltpu.VMEM((tokens, 2 * HEAD_WIDTH), F32),
        pltpu.VMEM((slots, tokens), F32),
        pltpu.VMEM((most, window), F32),
        pltpu.VMEM((max(most, slots), width), BF16),
        pltpu.VMEM((slots, half), F32),
        pltpu.VMEM((slots, half), BF16),
        pltpu.VMEM((slots, half), BF16),
        pltpu.VMEM((slots, half), BF16),
        pltpu.VMEM((slots, half), BF16),
        pltpu.VMEM((2, slots, half), BF16),
        pltpu.VMEM((slots, model), BF16),
        dma((3,)),
        dma((3,)),
        pltpu.VMEM(pieces, BF16),
        pltpu.VMEM(pieces, BF16),
        pltpu.VMEM(pieces, BF16),
        pltpu.VMEM(pieces, BF16),
        pltpu.VMEM(pieces, BF16),
        pltpu.VMEM(pieces, BF16),
        pltpu.VMEM(pieces, F32),
        dma((3, 2, PIECES)),
        dma((3, 2, PIECES)),
        pltpu.VMEM((2, slots, half), F32),
        pltpu.VMEM((slots, half), BF16),
        pltpu.VMEM((slots, half), BF16),
        pltpu.VMEM((slots, half), BF16),
        pltpu.VMEM((slots, half), BF16),
        pltpu.VMEM((2, slots, half), BF16),
        dma((3,)),
        dma((3,)),
    ]
    result = pl.pallas_call(
        functools.partial(layer_kernel, slots, parts),
        out_shape=jax.ShapeDtypeStruct((chunk, model), BF16),
        in_specs=[vmem] * 7 + [hbm] * 5,
        out_specs=vmem,
        scratch_shapes=scratch,
        compiler_params=pltpu.CompilerParams(
            collective_id=0, has_side_effects=True, vmem_limit_bytes=56 * 1024 * 1024
        ),
        cost_estimate=pl.CostEstimate(
            flops=14_000_000_000, bytes_accessed=14_000_000, transcendentals=7_000_000
        ),
    )(
        segment_ids[None, :], expert_ids.T, gate_weights.T, jnp.asarray(rotary_rows()),
        norm_gain[None, :], normed_key_heads, value_rows_per_head,
        query_heads, residual_in, out_weight, gate_up, down_weight,
    )
    return pl.pallas_call(
        hand_over,
        out_shape=jax.ShapeDtypeStruct((chunk, model), BF16),
        in_specs=[hbm],
        out_specs=hbm,
        scratch_shapes=[dma((COPIES,))],
    )(result)


def solution(mesh):
    placed = (
        P("req", "tp"),
        P("req", "tp"),
        P("req", "tp"),
        P(("req", "tp"), None),
        P("tp", None),
        P(),
        P(None, None, None, "tp"),
        P(None, "tp", None),
        P("req"),
        P("req", None),
        P("req", None),
    )
    return jax.shard_map(
        local, mesh=mesh, in_specs=placed, out_specs=P(("req", "tp"), None), check_vma=False
    )
```

```python
import functools
import math

import jax
import jax.numpy as jnp
import numpy as np
from jax import lax
from jax.experimental import pallas as pl
from jax.experimental.pallas import tpu as pltpu
from jax.sharding import PartitionSpec as P

QUERY_HEADS = 32
KEY_VALUE_HEADS = 4
HEAD_WIDTH = 128
EXPERTS = 128
SEG_MOST = 480
F32 = jnp.float32
BF16 = jnp.bfloat16
MASKED = -1e30
PIECES = 4
HEADS_AT_ONCE = 4
COPIES = 5
EXP2_SCALE = math.log2(math.e) / math.sqrt(HEAD_WIDTH)


def rotary_rows():
    half = HEAD_WIDTH // 2
    frequency = np.float32(1000000.0) ** (-np.arange(half, dtype=np.float32) / np.float32(half))
    angles = np.arange(SEG_MOST, dtype=np.float32)[:, None] * frequency[None, :].astype(np.float32)
    cosine, sine = np.cos(angles.astype(np.float64)), np.sin(angles.astype(np.float64))
    return np.concatenate([cosine, cosine, -sine, sine], axis=1).astype(np.float32)


def dot(a, b):
    return jnp.dot(a, b, preferred_element_type=F32)


def dot_nt(a, b):
    return lax.dot_general(a, b, (((1,), (1,)), ((), ())), preferred_element_type=F32)


def layer_kernel(
    slots, parts,
    seg_ref, ids_ref, gw_ref, table_ref, gain_ref, k_ref, v_ref,
    q_hbm, res_hbm, ow_hbm, gu_hbm, dw_hbm,
    out_ref,
    q, res, ow, gu, dw, load_sem,
    rows_ref, cols_ref, k_rot, v_ext, cs, bias_sel, bias, attended,
    sel_f, a1_send, a1_recv, a2_send, a2_recv, mixsel, xs, a_ssem, a_rsem,
    b1_send, b1_recv, b2_send, b2_recv, b3_send, b3_recv, own_f, b_ssem, b_rsem,
    y_f, c1_send, c1_recv, c2_send, c2_recv, ysum, c_ssem, c_rsem,
):
    me = lax.axis_index("tp")
    core = lax.rem(me, 2)
    chip = me // 2
    sib = chip * 2 + (1 - core)
    peer = (1 - chip) * 2 + core
    far = (1 - chip) * 2 + (1 - core)
    tokens, width = q.shape
    heads = width // HEAD_WIDTH
    chunk, model = out_ref.shape
    step = model // PIECES
    half = model // 2
    cap = slots // 2

    loads = [
        pltpu.make_async_copy(src, dst, load_sem.at[i])
        for i, (src, dst) in enumerate(
            [(q_hbm, q), (ow_hbm, ow), (res_hbm, res), (gu_hbm, gu), (dw_hbm, dw)]
        )
    ]
    for load in loads:
        load.start()

    barrier = pltpu.get_barrier_semaphore()
    for other in (sib, peer):
        pl.semaphore_signal(
            barrier, inc=1, device_id={"tp": other}, device_id_type=pl.DeviceIdType.MESH
        )

    def remote(src, dst, ssem, rsem, to):
        return pltpu.make_async_remote_copy(
            src_ref=src, dst_ref=dst, send_sem=ssem, recv_sem=rsem,
            device_id={"tp": to}, device_id_type=pl.DeviceIdType.MESH,
        )

    def remote_parts(i, src, dst, to):
        return [
            [
                remote(
                    src.at[s, p, pl.ds(0, rows)], dst.at[s, p, pl.ds(0, rows)],
                    b_ssem.at[i, s, p], b_rsem.at[i, s, p], to,
                )
                for p in range(PIECES)
            ]
            for s, (_, rows, _) in enumerate(parts)
        ]

    copy_a1 = remote(a1_send, a1_recv, a_ssem.at[0], a_rsem.at[0], sib)
    copy_a2 = remote(a2_send, a2_recv, a_ssem.at[1], a_rsem.at[1], peer)
    copy_a3 = remote(mixsel.at[core], mixsel.at[core], a_ssem.at[2], a_rsem.at[2], sib)
    copy_b1 = remote_parts(0, b1_send, b1_recv, sib)
    copy_b2 = remote_parts(1, b2_send, b2_recv, peer)
    copy_b3 = [
        remote(b3_send.at[p], b3_recv.at[p], b_ssem.at[2, 0, p], b_rsem.at[2, 0, p], sib)
        for p in range(PIECES)
    ]
    copy_c1 = remote(c1_send, c1_recv, c_ssem.at[0], c_rsem.at[0], sib)
    copy_c2 = remote(c2_send, c2_recv, c_ssem.at[1], c_rsem.at[1], peer)
    copy_c3 = remote(ysum.at[core], ysum.at[core], c_ssem.at[2], c_rsem.at[2], sib)

    seg = seg_ref[...]
    prompts = lax.broadcasted_iota(jnp.int32, (8, tokens), 0)
    starts = jnp.sum((seg < prompts).astype(F32), axis=1, keepdims=True)
    start_row = jnp.sum(jnp.where(seg == prompts, starts, 0.0), axis=0, keepdims=True)
    named = [ids_ref[...] == e for e in range(2)]
    chosen = [jnp.max(hit.astype(F32), axis=0, keepdims=True) for hit in named]
    route_rows = [jnp.sum(jnp.where(hit, gw_ref[...], 0.0), axis=0, keepdims=True) for hit in named]
    expert_at = lax.broadcasted_iota(jnp.int32, (16, tokens), 0)
    chosen = jnp.where(expert_at == 0, chosen[0], jnp.where(expert_at == 1, chosen[1], 0.0))
    upper = (
        lax.broadcasted_iota(jnp.int32, (128, 128), 0)
        < lax.broadcasted_iota(jnp.int32, (128, 128), 1)
    ).astype(F32).astype(BF16)
    rows_ref[...] = jnp.zeros_like(rows_ref)
    total = jnp.zeros((16, 1), F32)
    for low in range(0, tokens, 128):
        wide = min(128, tokens - low)
        block = chosen[:, low : low + wide]
        rank = dot(block.astype(BF16), upper[:wide, :wide]) + total
        total = total + jnp.sum(block, axis=1, keepdims=True)
        slot = jnp.where(block > 0, rank, -1.0)[:8]
        line = lax.broadcasted_iota(jnp.int32, (8, wide), 0)
        rows_ref[:, low : low + wide] = jnp.where(line == 2, start_row[:, low : low + wide], slot)
    cols_ref[...] = rows_ref[...].T

    table = table_ref[...]
    high = table.astype(BF16)
    low = (table - high.astype(F32)).astype(BF16)

    def rotary(position):
        places = lax.broadcasted_iota(jnp.int32, (position.shape[0], SEG_MOST), 1).astype(F32)
        at = (position == places).astype(F32).astype(BF16)
        return dot(at, high) + dot(at, low)

    def rotate(u, turn):
        u = u.astype(F32)
        turned = pltpu.roll(u, HEAD_WIDTH // 2, 1)
        return (u * turn[:, :HEAD_WIDTH] + turned * turn[:, HEAD_WIDTH:]).astype(BF16)

    token_col = lax.broadcasted_iota(jnp.int32, (tokens, 1), 0).astype(F32)
    cs[...] = rotary(token_col - cols_ref[:tokens, 2:3])
    k_rot[...] = rotate(k_ref[...], cs[...])
    v_ext[:, :HEAD_WIDTH] = v_ref[...]
    v_ext[:, HEAD_WIDTH:] = jnp.ones((tokens, HEAD_WIDTH), BF16)

    lane_tokens = lax.broadcasted_iota(jnp.int32, (cap, tokens), 1).astype(F32)
    slot_col = lax.broadcasted_iota(jnp.int32, (cap, tokens), 0).astype(F32)
    picks, routes, firsts, lasts, idents = [], [], [], [], []
    for e in range(2):
        hit = rows_ref[e : e + 1, :tokens] == slot_col
        picks.append(hit.astype(F32).astype(BF16))
        routes.append(jnp.sum(jnp.where(hit, route_rows[e], 0.0), axis=1, keepdims=True))
        first = jnp.sum(jnp.where(hit, start_row, 0.0), axis=1, keepdims=True)
        found = jnp.sum(jnp.where(hit, lane_tokens + 1.0, 0.0), axis=1, keepdims=True)
        last = jnp.maximum(found - 1.0, 0.0)
        keep = (lane_tokens >= first) & (lane_tokens <= last)
        bias_sel[e * cap : (e + 1) * cap, :] = jnp.where(keep, 0.0, MASKED)
        firsts.append(first)
        lasts.append(last)
        idents.append(found - 1.0)
    pick = jnp.concatenate(picks, axis=0)
    turn_sel = rotary(jnp.concatenate(lasts, axis=0) - jnp.concatenate(firsts, axis=0))
    loads[0].wait()
    q_sel = dot(pick, q[...])

    def attend(queries, keys, values, added):
        rows = added.shape[0]
        scores = dot_nt(jnp.concatenate(queries, axis=0), keys)
        weights = []
        for n in range(len(queries)):
            kept = scores[n * rows : (n + 1) * rows] + added
            peak = jnp.max(kept, axis=1, keepdims=True)
            weights.append(jnp.exp2((kept - peak) * EXP2_SCALE).astype(BF16))
        mixed = dot(jnp.concatenate(weights, axis=0), values)
        mixed = (mixed[:, :HEAD_WIDTH] / mixed[:, HEAD_WIDTH:]).astype(BF16)
        return [mixed[n * rows : (n + 1) * rows] for n in range(len(queries))]

    for low in range(0, heads, HEADS_AT_ONCE):
        lanes = [slice(h * HEAD_WIDTH, (h + 1) * HEAD_WIDTH) for h in range(low, low + HEADS_AT_ONCE)]
        queries = [rotate(q_sel[:, lane], turn_sel) for lane in lanes]
        for lane, got in zip(lanes, attend(queries, k_rot[...], v_ext[...], bias_sel[...])):
            attended[:slots, lane] = got
    loads[1].wait()
    loads[2].wait()
    own_tokens = (lax.broadcasted_iota(jnp.int32, (slots, chunk), 1) + me * chunk).astype(F32)
    own_pick = (own_tokens == jnp.concatenate(idents, axis=0)).astype(F32).astype(BF16)

    def chosen_share(side):
        columns = pl.ds(pl.multiple_of(side * half, half), half)
        return dot(attended[:slots, :], ow[:, columns]) + dot(own_pick, res[:, columns])

    a1_send[...] = chosen_share(1 - core).astype(BF16)
    pl.semaphore_wait(barrier, 2)
    copy_a1.start()
    sel_f[...] = chosen_share(core)

    def forward_a():
        copy_a1.wait_recv()
        a2_send[...] = (sel_f[...] + a1_recv[...].astype(F32)).astype(BF16)
        copy_a2.start()

    def attend_part(r, s, hooks=(), at=0):
        offset, rows, window = parts[s]
        base = pl.multiple_of(r * chunk + offset, 16)
        low = pl.multiple_of(jnp.maximum(r * chunk + (offset + rows - window), 0), 16)
        first = cols_ref[pl.ds(base, rows), 2:3]
        query_at = (lax.broadcasted_iota(jnp.int32, (rows, window), 0) + base).astype(F32)
        key_at = (lax.broadcasted_iota(jnp.int32, (rows, window), 1) + low).astype(F32)
        bias[:rows, :window] = jnp.where((key_at >= first) & (key_at <= query_at), 0.0, MASKED)

        def some_heads(i, carry):
            lanes = [
                pl.ds(pl.multiple_of((i * HEADS_AT_ONCE + n) * HEAD_WIDTH, HEAD_WIDTH), HEAD_WIDTH)
                for n in range(HEADS_AT_ONCE)
            ]
            turn = cs[pl.ds(base, rows), :]
            found = attend(
                [rotate(q[pl.ds(base, rows), lane], turn) for lane in lanes],
                k_rot[pl.ds(low, window), :],
                v_ext[pl.ds(low, window), :],
                bias[:rows, :window],
            )
            for lane, got in zip(lanes, found):
                attended[at : at + rows, lane] = got
            return carry

        turns = heads // HEADS_AT_ONCE
        if hooks:
            lax.fori_loop(0, turns // 2, some_heads, 0)
            hooks[0]()
            lax.fori_loop(turns // 2, turns, some_heads, 0)
            hooks[1]()
        else:
            lax.fori_loop(0, turns, some_heads, 0)

    def project(rows, p):
        return dot(attended[:rows, :], ow[:, p * step : (p + 1) * step])

    def send_far(s):
        rows = parts[s][1]
        for p in range(PIECES):
            b1_send[s, p, :rows] = project(rows, p).astype(BF16)
            copy_b1[s][p].start()

    def send_peer(s):
        rows = parts[s][1]
        for p in range(PIECES):
            share = project(rows, p)
            copy_b1[s][p].wait_recv()
            b2_send[s, p, :rows] = (share + b1_recv[s, p, :rows].astype(F32)).astype(BF16)
            copy_b2[s][p].start()

    def nothing():
        pass

    def experts():
        copy_a3.wait_recv()
        left, right = mixsel[0].astype(F32), mixsel[1].astype(F32)
        mean = (
            jnp.sum(left * left, axis=1, keepdims=True)
            + jnp.sum(right * right, axis=1, keepdims=True)
        ) / model
        scale = lax.rsqrt(mean + 1e-06)
        xs[:, :half] = (left * scale * gain_ref[:, :half]).astype(BF16)
        xs[:, half:] = (right * scale * gain_ref[:, half:]).astype(BF16)
        loads[3].wait()
        loads[4].wait()
        for e in range(2):
            rows = slice(e * cap, (e + 1) * cap)
            gate = dot_nt(xs[rows, :], gu[e, 0])
            upward = dot_nt(xs[rows, :], gu[e, 1])
            active = (gate / (1.0 + jnp.exp(-gate)) * upward).astype(BF16)
            for side in range(2):
                y_f[side, rows, :] = dot(active, dw[e, :, side * half : (side + 1) * half]) * routes[e]
        c1_send[...] = y_f[1 - core].astype(BF16)
        copy_c1.start()

    def forward_c():
        copy_c1.wait_recv()
        c2_send[...] = (y_f[core] + c1_recv[...].astype(F32)).astype(BF16)
        copy_c2.start()

    attend_part(far, 0, (forward_a, nothing))
    send_far(0)
    attend_part(peer, 0)
    send_peer(0)
    attend_part(far, 1)
    send_far(1)
    copy_a2.wait_recv()
    mixsel[core] = (a2_send[...].astype(F32) + a2_recv[...].astype(F32)).astype(BF16)
    copy_a3.start()
    attend_part(peer, 1, (experts, forward_c))
    send_peer(1)

    for s, (offset, _, _) in enumerate(parts):
        attend_part(sib, s, at=offset)
    for p in range(PIECES):
        b3_send[p] = project(chunk, p).astype(BF16)
        copy_b3[p].start()
    for s, (offset, _, _) in enumerate(parts):
        attend_part(me, s, at=offset)
    for p in range(PIECES):
        own_f[p] = project(chunk, p) + res[:, p * step : (p + 1) * step].astype(F32)

    copy_c2.wait_recv()
    ysum[core] = (c2_send[...].astype(F32) + c2_recv[...].astype(F32)).astype(BF16)
    copy_c3.start()
    for p in range(PIECES):
        copy_b3[p].wait_recv()
        own_f[p] = own_f[p] + b3_recv[p].astype(F32)
    copy_c3.wait_recv()
    for s, (offset, rows, _) in enumerate(parts):
        mine = pl.ds(pl.multiple_of(me * chunk + offset, 16), rows)
        slot_lane = lax.broadcasted_iota(jnp.int32, (rows, cap), 1).astype(F32)
        spread = [
            (cols_ref[mine, e : e + 1] == slot_lane).astype(F32).astype(BF16) for e in range(2)
        ]
        for p in range(PIECES):
            inner = p % (PIECES // 2) * step
            side = p * 2 // PIECES
            given = sum(
                dot(spread[e], ysum[side, e * cap : (e + 1) * cap, inner : inner + step])
                for e in range(2)
            )
            copy_b2[s][p].wait_recv()
            mixed = own_f[p, offset : offset + rows] + b2_recv[s, p, :rows].astype(F32)
            mixed = mixed.astype(BF16).astype(F32)
            out_ref[offset : offset + rows, p * step : (p + 1) * step] = (mixed + given).astype(BF16)

    for copy in [copy_a1, copy_a2, copy_a3, copy_c1, copy_c2, copy_c3] + copy_b3:
        copy.wait_send()
    for copies in copy_b1 + copy_b2:
        for copy in copies:
            copy.wait_send()


def hand_over(src, dst, held, sem):
    rows = src.shape[0] // COPIES
    spans = [pl.ds(i * rows, rows) for i in range(COPIES)]
    into = [
        pltpu.make_async_copy(src.at[span], held.at[span], sem.at[0, i])
        for i, span in enumerate(spans)
    ]
    out = [
        pltpu.make_async_copy(held.at[span], dst.at[span], sem.at[1, i])
        for i, span in enumerate(spans)
    ]
    for copy in into:
        copy.start()
    for first, second in zip(into, out):
        first.wait()
        second.start()
    for copy in out:
        copy.wait()


def local(
    query_heads,
    normed_key_heads,
    value_rows_per_head,
    residual_in,
    out_weight,
    norm_gain,
    gate_up,
    down_weight,
    segment_ids,
    expert_ids,
    gate_weights,
):
    tokens, width = query_heads.shape
    chunk, model = residual_in.shape
    capacity = tokens * expert_ids.shape[1] * 5 // (EXPERTS * 4)
    cap = -(-capacity // 16) * 16
    slots = 2 * cap
    first_rows = -(-chunk // 32) * 16
    parts = tuple(
        (offset, rows, min(tokens, -(-(rows + SEG_MOST - 1) // 16) * 16))
        for offset, rows in ((0, first_rows), (first_rows, chunk - first_rows))
    )
    most = max(rows for _, rows, _ in parts)
    window = max(wide for _, _, wide in parts)
    lanes = -(-tokens // 128) * 128


    vmem = pl.BlockSpec(memory_space=pltpu.VMEM)
    hbm = pl.BlockSpec(memory_space=pl.ANY)
    step = model // PIECES
    half = model // 2
    dma = pltpu.SemaphoreType.DMA
    pieces = (2, PIECES, most, step)
    whole = (PIECES, chunk, step)
    gate_up = jnp.swapaxes(gate_up, 2, 3)
    scratch = [
        pltpu.VMEM((tokens, width), BF16),
        pltpu.VMEM(residual_in.shape, BF16),
        pltpu.VMEM(out_weight.shape, BF16),
        pltpu.VMEM(gate_up.shape, BF16),
        pltpu.VMEM(down_weight.shape, BF16),
        dma((5,)),
        pltpu.VMEM((8, lanes), F32),
        pltpu.VMEM((lanes, 8), F32),
        pltpu.VMEM((tokens, HEAD_WIDTH), BF16),
        pltpu.VMEM((tokens, 2 * HEAD_WIDTH), BF16),
        pltpu.VMEM((tokens, 2 * HEAD_WIDTH), F32),
        pltpu.VMEM((slots, tokens), F32),
        pltpu.VMEM((most, window), F32),
        pltpu.VMEM((max(chunk, slots), width), BF16),
        pltpu.VMEM((slots, half), F32),
        pltpu.VMEM((slots, half), BF16),
        pltpu.VMEM((slots, half), BF16),
        pltpu.VMEM((slots, half), BF16),
        pltpu.VMEM((slots, half), BF16),
        pltpu.VMEM((2, slots, half), BF16),
        pltpu.VMEM((slots, model), BF16),
        dma((3,)),
        dma((3,)),
        pltpu.VMEM(pieces, BF16),
        pltpu.VMEM(pieces, BF16),
        pltpu.VMEM(pieces, BF16),
        pltpu.VMEM(pieces, BF16),
        pltpu.VMEM(whole, BF16),
        pltpu.VMEM(whole, BF16),
        pltpu.VMEM(whole, F32),
        dma((3, 2, PIECES)),
        dma((3, 2, PIECES)),
        pltpu.VMEM((2, slots, half), F32),
        pltpu.VMEM((slots, half), BF16),
        pltpu.VMEM((slots, half), BF16),
        pltpu.VMEM((slots, half), BF16),
        pltpu.VMEM((slots, half), BF16),
        pltpu.VMEM((2, slots, half), BF16),
        dma((3,)),
        dma((3,)),
    ]
    result = pl.pallas_call(
        functools.partial(layer_kernel, slots, parts),
        out_shape=jax.ShapeDtypeStruct((chunk, model), BF16),
        in_specs=[vmem] * 7 + [hbm] * 5,
        out_specs=vmem,
        scratch_shapes=scratch,
        compiler_params=pltpu.CompilerParams(
            collective_id=0, has_side_effects=True, vmem_limit_bytes=56 * 1024 * 1024
        ),
        cost_estimate=pl.CostEstimate(
            flops=14_000_000_000, bytes_accessed=14_000_000, transcendentals=7_000_000
        ),
    )(
        segment_ids[None, :], expert_ids.T, gate_weights.T, jnp.asarray(rotary_rows()),
        norm_gain[None, :], normed_key_heads, value_rows_per_head,
        query_heads, residual_in, out_weight, gate_up, down_weight,
    )
    return pl.pallas_call(
        hand_over,
        out_shape=jax.ShapeDtypeStruct((chunk, model), BF16),
        in_specs=[hbm],
        out_specs=hbm,
        scratch_shapes=[pltpu.VMEM((chunk, model), BF16), dma((2, COPIES))],
    )(result)


def solution(mesh):
    placed = (
        P("req", "tp"),
        P("req", "tp"),
        P("req", "tp"),
        P(("req", "tp"), None),
        P("tp", None),
        P(),
        P(None, None, None, "tp"),
        P(None, "tp", None),
        P("req"),
        P("req", None),
        P("req", None),
    )
    return jax.shard_map(
        local, mesh=mesh, in_specs=placed, out_specs=P(("req", "tp"), None), check_vma=False
    )
```

```python
import functools
import math

import jax
import jax.numpy as jnp
import numpy as np
from jax import lax
from jax.experimental import pallas as pl
from jax.experimental.pallas import tpu as pltpu
from jax.sharding import PartitionSpec as P

QUERY_HEADS = 32
KEY_VALUE_HEADS = 4
HEAD_WIDTH = 128
EXPERTS = 128
SEG_MOST = 480
F32 = jnp.float32
BF16 = jnp.bfloat16
MASKED = -1e30
PIECES = 4
HEADS_AT_ONCE = 4
COPIES = 5
EXP2_SCALE = math.log2(math.e) / math.sqrt(HEAD_WIDTH)


def rotary_rows():
    half = HEAD_WIDTH // 2
    frequency = np.float32(1000000.0) ** (-np.arange(half, dtype=np.float32) / np.float32(half))
    angles = np.arange(SEG_MOST, dtype=np.float32)[:, None] * frequency[None, :].astype(np.float32)
    cosine, sine = np.cos(angles.astype(np.float64)), np.sin(angles.astype(np.float64))
    return np.concatenate([cosine, cosine, -sine, sine], axis=1).astype(np.float32)


def dot(a, b):
    return jnp.dot(a, b, preferred_element_type=F32)


def dot_nt(a, b):
    return lax.dot_general(a, b, (((1,), (1,)), ((), ())), preferred_element_type=F32)


def layer_kernel(
    slots, parts,
    seg_ref, ids_ref, gw_ref, table_ref, gain_ref, k_ref, v_ref,
    q_hbm, res_hbm, ow_hbm, gu_hbm, dw_hbm,
    out_ref,
    out, given, out_sem,
    q, res, ow, gu, dw, load_sem,
    rows_ref, cols_ref, k_rot, v_ext, cs, bias_sel, bias, attended,
    sel_f, a1_send, a1_recv, a2_send, a2_recv, mixsel, xs, a_ssem, a_rsem,
    b1_send, b1_recv, b2_send, b2_recv, b3_send, b3_recv, own_f, b_ssem, b_rsem,
    y_f, c1_send, c1_recv, c2_send, c2_recv, ysum, c_ssem, c_rsem,
):
    me = lax.axis_index("tp")
    core = lax.rem(me, 2)
    chip = me // 2
    sib = chip * 2 + (1 - core)
    peer = (1 - chip) * 2 + core
    far = (1 - chip) * 2 + (1 - core)
    tokens, width = q.shape
    heads = width // HEAD_WIDTH
    chunk, model = out_ref.shape
    most = parts[0][1]
    step = model // PIECES
    half = model // 2
    cap = slots // 2

    loads = [
        pltpu.make_async_copy(src, dst, load_sem.at[i])
        for i, (src, dst) in enumerate(
            [(q_hbm, q), (ow_hbm, ow), (res_hbm, res), (gu_hbm, gu), (dw_hbm, dw)]
        )
    ]
    loads[0].start()

    barrier = pltpu.get_barrier_semaphore()
    for other in (sib, peer):
        pl.semaphore_signal(
            barrier, inc=1, device_id={"tp": other}, device_id_type=pl.DeviceIdType.MESH
        )

    def remote(src, dst, ssem, rsem, to):
        return pltpu.make_async_remote_copy(
            src_ref=src, dst_ref=dst, send_sem=ssem, recv_sem=rsem,
            device_id={"tp": to}, device_id_type=pl.DeviceIdType.MESH,
        )

    def remote_parts(i, src, dst, to):
        return [
            [
                remote(
                    src.at[s, p, pl.ds(0, rows)], dst.at[s, p, pl.ds(0, rows)],
                    b_ssem.at[i, s, p], b_rsem.at[i, s, p], to,
                )
                for p in range(PIECES)
            ]
            for s, (_, rows, _) in enumerate(parts)
        ]

    copy_a1 = remote(a1_send, a1_recv, a_ssem.at[0], a_rsem.at[0], sib)
    copy_a2 = remote(a2_send, a2_recv, a_ssem.at[1], a_rsem.at[1], peer)
    copy_a3 = remote(mixsel.at[core], mixsel.at[core], a_ssem.at[2], a_rsem.at[2], sib)
    copy_b1 = remote_parts(0, b1_send, b1_recv, sib)
    copy_b2 = remote_parts(1, b2_send, b2_recv, peer)
    copy_b3 = [
        remote(b3_send.at[p], b3_recv.at[p], b_ssem.at[2, 0, p], b_rsem.at[2, 0, p], sib)
        for p in range(PIECES)
    ]
    copy_c1 = remote(c1_send, c1_recv, c_ssem.at[0], c_rsem.at[0], sib)
    copy_c2 = remote(c2_send, c2_recv, c_ssem.at[1], c_rsem.at[1], peer)
    copy_c3 = remote(ysum.at[core], ysum.at[core], c_ssem.at[2], c_rsem.at[2], sib)

    loads[1].start()
    loads[2].start()

    seg = seg_ref[...]
    prompts = lax.broadcasted_iota(jnp.int32, (8, tokens), 0)
    starts = jnp.sum((seg < prompts).astype(F32), axis=1, keepdims=True)
    start_row = jnp.sum(jnp.where(seg == prompts, starts, 0.0), axis=0, keepdims=True)
    named = [ids_ref[...] == e for e in range(2)]
    chosen = [jnp.max(hit.astype(F32), axis=0, keepdims=True) for hit in named]
    route_rows = [jnp.sum(jnp.where(hit, gw_ref[...], 0.0), axis=0, keepdims=True) for hit in named]
    expert_at = lax.broadcasted_iota(jnp.int32, (16, tokens), 0)
    chosen = jnp.where(expert_at == 0, chosen[0], jnp.where(expert_at == 1, chosen[1], 0.0))
    upper = (
        lax.broadcasted_iota(jnp.int32, (128, 128), 0)
        < lax.broadcasted_iota(jnp.int32, (128, 128), 1)
    ).astype(F32).astype(BF16)
    rows_ref[...] = jnp.zeros_like(rows_ref)
    total = jnp.zeros((16, 1), F32)
    for low in range(0, tokens, 128):
        wide = min(128, tokens - low)
        block = chosen[:, low : low + wide]
        rank = dot(block.astype(BF16), upper[:wide, :wide]) + total
        total = total + jnp.sum(block, axis=1, keepdims=True)
        slot = jnp.where(block > 0, rank, -1.0)[:8]
        line = lax.broadcasted_iota(jnp.int32, (8, wide), 0)
        rows_ref[:, low : low + wide] = jnp.where(line == 2, start_row[:, low : low + wide], slot)
    cols_ref[...] = rows_ref[...].T

    table = table_ref[...]
    high = table.astype(BF16)
    low = (table - high.astype(F32)).astype(BF16)

    def rotary(position):
        places = lax.broadcasted_iota(jnp.int32, (position.shape[0], SEG_MOST), 1).astype(F32)
        at = (position == places).astype(F32).astype(BF16)
        return dot(at, high) + dot(at, low)

    def rotate(u, turn):
        u = u.astype(F32)
        turned = pltpu.roll(u, HEAD_WIDTH // 2, 1)
        return (u * turn[:, :HEAD_WIDTH] + turned * turn[:, HEAD_WIDTH:]).astype(BF16)

    token_col = lax.broadcasted_iota(jnp.int32, (tokens, 1), 0).astype(F32)
    cs[...] = rotary(token_col - cols_ref[:tokens, 2:3])
    k_rot[...] = rotate(k_ref[...], cs[...])
    v_ext[:, :HEAD_WIDTH] = v_ref[...]
    v_ext[:, HEAD_WIDTH:] = jnp.ones((tokens, HEAD_WIDTH), BF16)

    lane_tokens = lax.broadcasted_iota(jnp.int32, (cap, tokens), 1).astype(F32)
    slot_col = lax.broadcasted_iota(jnp.int32, (cap, tokens), 0).astype(F32)
    picks, routes, firsts, lasts, idents = [], [], [], [], []
    for e in range(2):
        hit = rows_ref[e : e + 1, :tokens] == slot_col
        picks.append(hit.astype(F32).astype(BF16))
        routes.append(jnp.sum(jnp.where(hit, route_rows[e], 0.0), axis=1, keepdims=True))
        first = jnp.sum(jnp.where(hit, start_row, 0.0), axis=1, keepdims=True)
        found = jnp.sum(jnp.where(hit, lane_tokens + 1.0, 0.0), axis=1, keepdims=True)
        last = jnp.maximum(found - 1.0, 0.0)
        keep = (lane_tokens >= first) & (lane_tokens <= last)
        bias_sel[e * cap : (e + 1) * cap, :] = jnp.where(keep, 0.0, MASKED)
        firsts.append(first)
        lasts.append(last)
        idents.append(found - 1.0)
    pick = jnp.concatenate(picks, axis=0)
    turn_sel = rotary(jnp.concatenate(lasts, axis=0) - jnp.concatenate(firsts, axis=0))
    loads[0].wait()
    q_sel = dot(pick, q[...])

    def attend(queries, keys, values, added):
        rows = added.shape[0]
        scores = dot_nt(jnp.concatenate(queries, axis=0), keys)
        weights = []
        for n in range(len(queries)):
            kept = scores[n * rows : (n + 1) * rows] + added
            peak = jnp.max(kept, axis=1, keepdims=True)
            weights.append(jnp.exp2((kept - peak) * EXP2_SCALE).astype(BF16))
        mixed = dot(jnp.concatenate(weights, axis=0), values)
        mixed = (mixed[:, :HEAD_WIDTH] / mixed[:, HEAD_WIDTH:]).astype(BF16)
        return [mixed[n * rows : (n + 1) * rows] for n in range(len(queries))]

    for low in range(0, heads, HEADS_AT_ONCE):
        lanes = [slice(h * HEAD_WIDTH, (h + 1) * HEAD_WIDTH) for h in range(low, low + HEADS_AT_ONCE)]
        queries = [rotate(q_sel[:, lane], turn_sel) for lane in lanes]
        for lane, got in zip(lanes, attend(queries, k_rot[...], v_ext[...], bias_sel[...])):
            attended[:slots, lane] = got
    loads[1].wait()
    loads[2].wait()
    loads[3].start()
    loads[4].start()
    own_tokens = (lax.broadcasted_iota(jnp.int32, (slots, chunk), 1) + me * chunk).astype(F32)
    own_pick = (own_tokens == jnp.concatenate(idents, axis=0)).astype(F32).astype(BF16)

    def chosen_share(side):
        columns = pl.ds(pl.multiple_of(side * half, half), half)
        return dot(attended[:slots, :], ow[:, columns]) + dot(own_pick, res[:, columns])

    a1_send[...] = chosen_share(1 - core).astype(BF16)
    pl.semaphore_wait(barrier, 2)
    copy_a1.start()
    sel_f[...] = chosen_share(core)

    def forward_a():
        copy_a1.wait_recv()
        a2_send[...] = (sel_f[...] + a1_recv[...].astype(F32)).astype(BF16)
        copy_a2.start()

    def attend_part(r, s, hooks=(), at=0):
        offset, rows, window = parts[s]
        base = pl.multiple_of(r * chunk + offset, 16)
        low = pl.multiple_of(jnp.maximum(r * chunk + (offset + rows - window), 0), 16)
        first = cols_ref[pl.ds(base, rows), 2:3]
        query_at = (lax.broadcasted_iota(jnp.int32, (rows, window), 0) + base).astype(F32)
        key_at = (lax.broadcasted_iota(jnp.int32, (rows, window), 1) + low).astype(F32)
        bias[:rows, :window] = jnp.where((key_at >= first) & (key_at <= query_at), 0.0, MASKED)

        def some_heads(i, carry):
            lanes = [
                pl.ds(pl.multiple_of((i * HEADS_AT_ONCE + n) * HEAD_WIDTH, HEAD_WIDTH), HEAD_WIDTH)
                for n in range(HEADS_AT_ONCE)
            ]
            turn = cs[pl.ds(base, rows), :]
            found = attend(
                [rotate(q[pl.ds(base, rows), lane], turn) for lane in lanes],
                k_rot[pl.ds(low, window), :],
                v_ext[pl.ds(low, window), :],
                bias[:rows, :window],
            )
            for lane, got in zip(lanes, found):
                attended[at : at + rows, lane] = got
            return carry

        turns = heads // HEADS_AT_ONCE
        if hooks:
            lax.fori_loop(0, turns // 2, some_heads, 0)
            hooks[0]()
            lax.fori_loop(turns // 2, turns, some_heads, 0)
            hooks[1]()
        else:
            lax.fori_loop(0, turns, some_heads, 0)

    def project(rows, p, at=0):
        return dot(attended[at : at + rows, :], ow[:, p * step : (p + 1) * step])

    def send_far(s):
        rows = parts[s][1]
        for p in range(PIECES):
            b1_send[s, p, :rows] = project(rows, p).astype(BF16)
            copy_b1[s][p].start()

    def send_peer(s, at_once):
        rows = parts[s][1]
        for p in range(PIECES):
            share = project(rows, p)
            copy_b1[s][p].wait_recv()
            b2_send[s, p, :rows] = (share + b1_recv[s, p, :rows].astype(F32)).astype(BF16)
            if p < at_once:
                copy_b2[s][p].start()

    def nothing():
        pass

    def experts():
        copy_a3.wait_recv()
        left, right = mixsel[0].astype(F32), mixsel[1].astype(F32)
        mean = (
            jnp.sum(left * left, axis=1, keepdims=True)
            + jnp.sum(right * right, axis=1, keepdims=True)
        ) / model
        scale = lax.rsqrt(mean + 1e-06)
        xs[:, :half] = (left * scale * gain_ref[:, :half]).astype(BF16)
        xs[:, half:] = (right * scale * gain_ref[:, half:]).astype(BF16)
        loads[3].wait()
        loads[4].wait()
        for e in range(2):
            rows = slice(e * cap, (e + 1) * cap)
            gate = dot_nt(xs[rows, :], gu[e, 0])
            upward = dot_nt(xs[rows, :], gu[e, 1])
            active = (gate / (1.0 + jnp.exp(-gate)) * upward).astype(BF16)
            for side in range(2):
                y_f[side, rows, :] = dot(active, dw[e, :, side * half : (side + 1) * half]) * routes[e]
        c1_send[...] = y_f[1 - core].astype(BF16)
        copy_c1.start()

    def forward_c():
        copy_c1.wait_recv()
        c2_send[...] = (y_f[core] + c1_recv[...].astype(F32)).astype(BF16)
        copy_c2.start()

    attend_part(far, 0, (forward_a, nothing))
    send_far(0)
    attend_part(peer, 0)
    send_peer(0, PIECES)
    attend_part(far, 1)
    send_far(1)
    copy_a2.wait_recv()
    mixsel[core] = (a2_send[...].astype(F32) + a2_recv[...].astype(F32)).astype(BF16)
    copy_a3.start()
    attend_part(sib, 0, (experts, forward_c), at=most)
    attend_part(peer, 1)
    send_peer(1, 1)
    attend_part(sib, 1, at=most + parts[1][0])
    copy_c2.wait_send()
    for copy in copy_b2[1][1:]:
        copy.start()
    for p in range(PIECES):
        b3_send[p] = project(chunk, p, most).astype(BF16)
        copy_b3[p].start()
    for s, (offset, _, _) in enumerate(parts):
        attend_part(me, s, at=offset)
    for p in range(PIECES):
        own_f[p] = project(chunk, p) + res[:, p * step : (p + 1) * step].astype(F32)

    copy_c2.wait_recv()
    ysum[core] = (c2_send[...].astype(F32) + c2_recv[...].astype(F32)).astype(BF16)
    copy_c3.start()
    for p in range(PIECES):
        copy_b3[p].wait_recv()
        own_f[p] = own_f[p] + b3_recv[p].astype(F32)
    mine = pl.ds(pl.multiple_of(me * chunk, 16), chunk)
    slot_lane = lax.broadcasted_iota(jnp.int32, (chunk, cap), 1).astype(F32)
    spread = jnp.concatenate(
        [(cols_ref[mine, e : e + 1] == slot_lane).astype(F32).astype(BF16) for e in range(2)], axis=1
    )
    copy_c3.wait_recv()
    for p in range(PIECES):
        inner = p % (PIECES // 2) * step
        given[p] = dot(spread, ysum[p * 2 // PIECES, :, inner : inner + step])
    written = []
    for s, (offset, rows, _) in enumerate(parts):
        span = slice(offset, offset + rows)
        for p in range(PIECES):
            copy_b2[s][p].wait_recv()
            mixed = own_f[p, span] + b2_recv[s, p, :rows].astype(F32)
            mixed = mixed.astype(BF16).astype(F32)
            columns = pl.ds(p * step, step)
            out[span, p * step : (p + 1) * step] = (mixed + given[p, span]).astype(BF16)
            done = pltpu.make_async_copy(
                out.at[pl.ds(offset, rows), columns],
                out_ref.at[pl.ds(offset, rows), columns],
                out_sem.at[s, p],
            )
            done.start()
            written.append(done)

    for copy in [copy_a1, copy_a2, copy_a3, copy_c1, copy_c3] + copy_b3:
        copy.wait_send()
    for copies in copy_b1 + copy_b2:
        for copy in copies:
            copy.wait_send()
    for done in written:
        done.wait()


def hand_over(src, dst, held, sem):
    rows = src.shape[0] // COPIES
    spans = [pl.ds(i * rows, rows) for i in range(COPIES)]
    into = [
        pltpu.make_async_copy(src.at[span], held.at[span], sem.at[0, i])
        for i, span in enumerate(spans)
    ]
    out = [
        pltpu.make_async_copy(held.at[span], dst.at[span], sem.at[1, i])
        for i, span in enumerate(spans)
    ]
    for copy in into:
        copy.start()
    for first, second in zip(into, out):
        first.wait()
        second.start()
    for copy in out:
        copy.wait()


def local(
    query_heads,
    normed_key_heads,
    value_rows_per_head,
    residual_in,
    out_weight,
    norm_gain,
    gate_up,
    down_weight,
    segment_ids,
    expert_ids,
    gate_weights,
):
    tokens, width = query_heads.shape
    chunk, model = residual_in.shape
    capacity = tokens * expert_ids.shape[1] * 5 // (EXPERTS * 4)
    cap = -(-capacity // 16) * 16
    slots = 2 * cap
    first_rows = -(-chunk // 32) * 16
    parts = tuple(
        (offset, rows, min(tokens, -(-(rows + SEG_MOST - 1) // 16) * 16))
        for offset, rows in ((0, first_rows), (first_rows, chunk - first_rows))
    )
    most = max(rows for _, rows, _ in parts)
    window = max(wide for _, _, wide in parts)
    lanes = -(-tokens // 128) * 128


    vmem = pl.BlockSpec(memory_space=pltpu.VMEM)
    hbm = pl.BlockSpec(memory_space=pl.ANY)
    step = model // PIECES
    half = model // 2
    dma = pltpu.SemaphoreType.DMA
    pieces = (2, PIECES, most, step)
    whole = (PIECES, chunk, step)
    gate_up = jnp.swapaxes(gate_up, 2, 3)
    scratch = [
        pltpu.VMEM((chunk, model), BF16),
        pltpu.VMEM(whole, F32),
        dma((2, PIECES)),
        pltpu.VMEM((tokens, width), BF16),
        pltpu.VMEM(residual_in.shape, BF16),
        pltpu.VMEM(out_weight.shape, BF16),
        pltpu.VMEM(gate_up.shape, BF16),
        pltpu.VMEM(down_weight.shape, BF16),
        dma((5,)),
        pltpu.VMEM((8, lanes), F32),
        pltpu.VMEM((lanes, 8), F32),
        pltpu.VMEM((tokens, HEAD_WIDTH), BF16),
        pltpu.VMEM((tokens, 2 * HEAD_WIDTH), BF16),
        pltpu.VMEM((tokens, 2 * HEAD_WIDTH), F32),
        pltpu.VMEM((slots, tokens), F32),
        pltpu.VMEM((most, window), F32),
        pltpu.VMEM((max(most + chunk, slots), width), BF16),
        pltpu.VMEM((slots, half), F32),
        pltpu.VMEM((slots, half), BF16),
        pltpu.VMEM((slots, half), BF16),
        pltpu.VMEM((slots, half), BF16),
        pltpu.VMEM((slots, half), BF16),
        pltpu.VMEM((2, slots, half), BF16),
        pltpu.VMEM((slots, model), BF16),
        dma((3,)),
        dma((3,)),
        pltpu.VMEM(pieces, BF16),
        pltpu.VMEM(pieces, BF16),
        pltpu.VMEM(pieces, BF16),
        pltpu.VMEM(pieces, BF16),
        pltpu.VMEM(whole, BF16),
        pltpu.VMEM(whole, BF16),
        pltpu.VMEM(whole, F32),
        dma((3, 2, PIECES)),
        dma((3, 2, PIECES)),
        pltpu.VMEM((2, slots, half), F32),
        pltpu.VMEM((slots, half), BF16),
        pltpu.VMEM((slots, half), BF16),
        pltpu.VMEM((slots, half), BF16),
        pltpu.VMEM((slots, half), BF16),
        pltpu.VMEM((2, slots, half), BF16),
        dma((3,)),
        dma((3,)),
    ]
    result = pl.pallas_call(
        functools.partial(layer_kernel, slots, parts),
        out_shape=jax.ShapeDtypeStruct((chunk, model), BF16),
        in_specs=[vmem] * 7 + [hbm] * 5,
        out_specs=hbm,
        scratch_shapes=scratch,
        compiler_params=pltpu.CompilerParams(
            collective_id=0, has_side_effects=True, vmem_limit_bytes=56 * 1024 * 1024
        ),
        cost_estimate=pl.CostEstimate(
            flops=14_000_000_000, bytes_accessed=14_000_000, transcendentals=7_000_000
        ),
    )(
        segment_ids[None, :], expert_ids.T, gate_weights.T, jnp.asarray(rotary_rows()),
        norm_gain[None, :], normed_key_heads, value_rows_per_head,
        query_heads, residual_in, out_weight, gate_up, down_weight,
    )
    return pl.pallas_call(
        hand_over,
        out_shape=jax.ShapeDtypeStruct((chunk, model), BF16),
        in_specs=[hbm],
        out_specs=hbm,
        scratch_shapes=[pltpu.VMEM((chunk, model), BF16), dma((2, COPIES))],
    )(result)


def solution(mesh):
    placed = (
        P("req", "tp"),
        P("req", "tp"),
        P("req", "tp"),
        P(("req", "tp"), None),
        P("tp", None),
        P(),
        P(None, None, None, "tp"),
        P(None, "tp", None),
        P("req"),
        P("req", None),
        P("req", None),
    )
    return jax.shard_map(
        local, mesh=mesh, in_specs=placed, out_specs=P(("req", "tp"), None), check_vma=False
    )
```
